256 devices in a mesh: ctx: 32 (over x_lo, z, core), head: 8 (over x_hi, y).
Axes of the slice: x: 4 (x_hi: 2, x_lo: 2; x = x_hi * 2 + x_lo), y: 4, z: 8, core: 2. Of those that a mesh axis runs over, the one named last changes fastest.
Arguments:
- queries: bfloat16 [8192, 8192], P('ctx', 'head'), may hold values from -6 to 6
- keys: bfloat16 [8192, 1024], P('ctx', 'head'), may hold values from -6 to 6
- values: bfloat16 [8192, 1024], P('ctx', 'head'), may hold values from -6 to 6
- doc_lengths: int32 [16], replicated, may hold values from 1 to 4096, 8192 in all
- span_order: int32 [64], replicated, may hold values from 0 to 63, each once
Outputs:
- attended: bfloat16 [8192, 8192], P(('ctx', 'head'))
The draws below stay inside these ranges and needn't reach their ends.
Inputs may be any that keep to these rules, and one draw needn't show every extreme that they name: `doc_lengths`: every document has at least one token and they fill the sequence; the longest has exactly 4096. `span_order`: each span appears in exactly one slot.
All inputs are finite; a program needn't handle non-finite values.
Results may differ from the reference program's by a relative error of at most 0.004.
Values may be sent and summed in bfloat16 or wider, within the bound.
A program may use at most 192 MiB of HBM per device.

```python
import math
import jax
import jax.numpy as jnp
import numpy as np
from jax import lax

HD = 128
NDOCS = 16
KVH = 8
QHEADS = 64
SEQ = 8192
CH = 128
NCHUNK = 64
DOC_MOST = 4096


def draw_keys(key, part):
    base = jnp.clip(jax.random.normal(jax.random.fold_in(key, 1), (SEQ, KVH * HD), jnp.float32), -4.0, 4.0)
    return base.astype(jnp.bfloat16)


def draw_queries(key, part):
    base = jnp.clip(jax.random.normal(jax.random.fold_in(key, 2), (SEQ, QHEADS * HD), jnp.float32), -4.0, 4.0)
    return base.astype(jnp.bfloat16)


def draw_values(key, part):
    noise = jnp.clip(jax.random.normal(jax.random.fold_in(key, 3), (SEQ, KVH * HD), jnp.float32), -4.0, 4.0)
    offset = jnp.clip(jax.random.normal(jax.random.fold_in(key, 4), (SEQ // CH, KVH * HD), jnp.float32), -2.5, 2.5)
    return (0.7 * noise + 0.8 * jnp.repeat(offset, CH, axis=0)).astype(jnp.bfloat16)


def split_up(amount, total, limit, lean):
    portions = [(1 << 20) // math.isqrt(standing ** lean) + 1 for standing in range(2, amount + 1)]
    rest, holding = total - limit - (amount - 1), [1] * (amount - 1)
    while rest > 0:
        free = [i for i in range(amount - 1) if holding[i] < limit]
        mass, budget = sum([portions[i] for i in free]), rest
        for i in free:
            extra = min(limit - holding[i], max(1, budget * portions[i] // mass), rest)
            holding[i] = holding[i] + extra
            rest = rest - extra
    return np.array([limit] + holding)


def uneven_parts(rng, count, total, most, slope):
    if count == 2:
        one = jax.random.randint(rng, (), max(1, total - most), min(most, total - 1) + 1)
        return jnp.stack([one, total - one])
    lengths = jnp.asarray(split_up(count, total, most, slope), jnp.int32)
    pairs = (count - 1) // 2
    donor, taker = lengths[1:1 + 2 * pairs:2], lengths[2:2 + 2 * pairs:2]
    margin = jnp.minimum(donor - 1, most - taker)
    shifted = jax.random.randint(jax.random.fold_in(rng, 1), (pairs,), 0, 1 << 20) % (margin + 1)
    lengths = lengths.at[1:1 + 2 * pairs:2].set(donor - shifted).at[2:2 + 2 * pairs:2].set(taker + shifted)
    return lengths[jax.random.permutation(jax.random.fold_in(rng, 2), count)]


def setup_inputs(seed: int = 0) -> dict:
    streams_of = jax.random.split(jax.random.key(seed), 6)
    queries = draw_queries(jax.random.fold_in(streams_of[5], 71), 0)
    keys = draw_keys(jax.random.fold_in(streams_of[5], 71), 0)
    values = draw_values(jax.random.fold_in(streams_of[5], 71), 0)
    doc_lengths = uneven_parts(streams_of[3], NDOCS, SEQ, DOC_MOST, 2).astype(jnp.int32)
    span_order = jax.random.permutation(streams_of[4], NCHUNK).astype(jnp.int32)
    return {"queries": queries, "keys": keys, "values": values, "doc_lengths": doc_lengths, "span_order": span_order}


def reference(queries, keys, values, doc_lengths, span_order):
    seqlen = queries.shape[0]
    nchunk = span_order.shape[0]
    span = seqlen // nchunk
    qheads = queries.shape[1] // HD
    kvheads = keys.shape[1] // HD
    group = qheads // kvheads
    rows = jnp.arange(seqlen, dtype=jnp.int32)
    pos = (span_order[rows // span] * span + rows % span).astype(jnp.int32)
    ends = jnp.cumsum(doc_lengths).astype(jnp.int32)
    doc = lax.optimization_barrier(jnp.sum((pos[:, None] >= ends[None, :]).astype(jnp.int32), axis=1))
    key_f = keys.astype(jnp.float32).reshape(seqlen, kvheads, HD)
    val_f = values.astype(jnp.float32).reshape(seqlen, kvheads, HD)
    block = math.gcd(seqlen, 128)
    scale = 1.0 / math.sqrt(HD)
    q_blocks = queries.reshape(seqlen // block, block, kvheads, group, HD)

    def one(args):
        q_blk, p_blk, d_blk = args
        score = jnp.einsum('qcgd,kcd->cgqk', q_blk.astype(jnp.float32), key_f) * scale
        allowed = (d_blk[:, None] == doc[None, :]) & (pos[None, :] <= p_blk[:, None])
        masked = jnp.where(allowed[None, None], score, -1e+30)
        top = lax.optimization_barrier(jnp.max(masked, axis=-1, keepdims=True))
        weight = jnp.where(allowed[None, None], jnp.exp(score - top), 0.0)
        total = lax.optimization_barrier(jnp.sum(weight, axis=-1))
        weight_b = lax.optimization_barrier(weight.astype(jnp.bfloat16)).astype(jnp.float32)
        out = jnp.einsum('cgqk,kcd->cgqd', weight_b, val_f) / total[..., None]
        return jnp.transpose(out, (2, 0, 1, 3)).reshape(block, qheads * HD).astype(jnp.bfloat16)
    out = lax.map(one, (q_blocks, pos.reshape(-1, block), doc.reshape(-1, block)))
    return out.reshape(seqlen, qheads * HD)
```

```python
import functools
import math

import jax
import jax.numpy as jnp
from jax import lax
from jax.experimental import pallas as pl
from jax.experimental.pallas import tpu as pltpu
from jax.sharding import PartitionSpec as P

HD = 128
SPAN = 128
MOST = 4096
CHUNK = 256


def doc_start(lengths_ref, ndocs, pos):
    start, end = jnp.int32(0), jnp.int32(0)
    for d in range(ndocs):
        end = end + lengths_ref[d]
        start = jnp.where(pos >= end, end, start)
    return start


def attend_kernel(
    lengths_ref, order_ref, q_ref, kv_ref, out_ref,
    inverse, q_st, keys, vals, top, accum, bias, sems,
):
    ndocs = lengths_ref.shape[0]
    nspan = order_ref.shape[0]
    spans = q_ref.shape[0] // SPAN
    heads = q_ref.shape[1] // HD
    per = CHUNK // SPAN
    me = lax.axis_index("ctx")
    rate = math.log2(math.e) / math.sqrt(HD)

    @pl.loop(0, nspan)
    def _(i):
        inverse[order_ref[i]] = i

    def fetch(t, c, i):
        for j in range(per):
            slot = inverse[c * per + j]
            src = kv_ref.at[pl.ds(pl.multiple_of(slot * SPAN, SPAN), SPAN)]
            dst = pl.ds(pl.multiple_of(i * CHUNK + j * SPAN, SPAN), SPAN)
            pltpu.make_async_copy(src.at[:, :HD], keys.at[t, dst], sems.at[t, i, 0]).start()
            pltpu.make_async_copy(src.at[:, HD:], vals.at[t, dst, :HD], sems.at[t, i, 1]).start()

    last, count, whole = [], [], []
    for t in range(spans):
        p = order_ref[me * spans + t]
        first = doc_start(lengths_ref, ndocs, p * SPAN)
        inner = doc_start(lengths_ref, ndocs, p * SPAN + SPAN - 1)
        last.append(p)
        count.append(p // per - first // CHUNK + 1)
        whole.append(inner)

        @pl.loop(0, count[t])
        def _(i):
            fetch(t, p // per - i, i)

    for t in range(spans):
        for h in range(heads):
            q_st[t, h * SPAN : (h + 1) * SPAN] = q_ref[
                t * SPAN : (t + 1) * SPAN, h * HD : (h + 1) * HD
            ]
        vals[t, :, HD:] = jnp.ones((vals.shape[1], HD), jnp.bfloat16)

    for t in range(spans):
        p = last[t]
        row_pos = p * SPAN + lax.broadcasted_iota(jnp.int32, (SPAN, HD), 0)
        row_start = jnp.zeros((SPAN, HD), jnp.int32)
        end = jnp.int32(0)
        for d in range(ndocs):
            end = end + lengths_ref[d]
            row_start = jnp.where(row_pos >= end, end, row_start)

        def fold(i, masked, begin):
            rows = pl.ds(pl.multiple_of(i * CHUNK, CHUNK), CHUNK)
            if masked:
                for j in range(CHUNK // HD):
                    col = (p // per - i) * CHUNK + j * HD + lax.broadcasted_iota(
                        jnp.int32, (SPAN, HD), 1
                    )
                    ok = (col >= row_start) & (col <= row_pos)
                    bias[:, j * HD : (j + 1) * HD] = jnp.where(ok, 0.0, -1e30)
            kb = keys[t, rows]
            vb = vals[t, rows]
            for h in range(0, heads, 2):
                part = pl.ds(h * SPAN, 2 * SPAN)
                score = lax.dot_general(
                    q_st[t, part], kb, (((1,), (1,)), ((), ())),
                    preferred_element_type=jnp.float32,
                ) * rate
                if masked:
                    score = (score.reshape(2, SPAN, CHUNK) + bias[...][None]).reshape(2 * SPAN, CHUNK)
                best = jnp.max(score, axis=1, keepdims=True)
                if begin:
                    fresh = jnp.broadcast_to(best, (2 * SPAN, HD))
                else:
                    old = top[part]
                    fresh = jnp.maximum(old, best)
                weight = jnp.exp2(score - jnp.concatenate([fresh] * (CHUNK // HD), axis=1))
                made = jnp.dot(
                    weight.astype(jnp.bfloat16), vb, preferred_element_type=jnp.float32
                )
                top[part] = fresh
                if begin:
                    accum[part] = made
                else:
                    factor = jnp.exp2(old - fresh)
                    accum[part] = accum[part] * jnp.concatenate([factor, factor], axis=1) + made

        def arrive(i):
            rows = pl.ds(pl.multiple_of(i * CHUNK, CHUNK), CHUNK)
            pltpu.make_async_copy(kv_ref.at[pl.ds(0, CHUNK), :HD], keys.at[t, rows], sems.at[t, i, 0]).wait()
            pltpu.make_async_copy(kv_ref.at[pl.ds(0, CHUNK), HD:], vals.at[t, rows, :HD], sems.at[t, i, 1]).wait()

        arrive(0)
        fold(0, True, True)

        @pl.loop(1, count[t])
        def _(i):
            arrive(i)
            clear = (p // per - i) * CHUNK >= whole[t]

            @pl.when(clear)
            def _():
                fold(i, False, False)

            @pl.when(jnp.logical_not(clear))
            def _():
                fold(i, True, False)

        for h in range(heads):
            part = pl.ds(h * SPAN, SPAN)
            done = accum[part, :HD] / accum[part, HD:]
            out_ref[t * SPAN : (t + 1) * SPAN, h * HD : (h + 1) * HD] = done.astype(jnp.bfloat16)


def attend(queries, kv, doc_lengths, span_order):
    rows, width = queries.shape
    heads, spans = width // HD, rows // SPAN
    chunks = MOST // CHUNK + 1
    smem = pl.BlockSpec(memory_space=pltpu.SMEM)
    return pl.pallas_call(
        attend_kernel,
        out_shape=jax.ShapeDtypeStruct((rows, width), jnp.bfloat16),
        in_specs=[smem, smem, pl.BlockSpec(memory_space=pltpu.VMEM), pl.BlockSpec(memory_space=pl.ANY)],
        out_specs=pl.BlockSpec(memory_space=pltpu.VMEM),
        scratch_shapes=[
            pltpu.SMEM((span_order.shape[0],), jnp.int32),
            pltpu.VMEM((spans, heads * SPAN, HD), jnp.bfloat16),
            pltpu.VMEM((spans, chunks * CHUNK, HD), jnp.bfloat16),
            pltpu.VMEM((spans, chunks * CHUNK, 2 * HD), jnp.bfloat16),
            pltpu.VMEM((heads * SPAN, HD), jnp.float32),
            pltpu.VMEM((heads * SPAN, 2 * HD), jnp.float32),
            pltpu.VMEM((SPAN, CHUNK), jnp.float32),
            pltpu.SemaphoreType.DMA((spans, chunks, 2)),
        ],
        compiler_params=pltpu.CompilerParams(vmem_limit_bytes=40 * 2**20),
        name="attend",
    )(doc_lengths, span_order, queries, kv)


def body(queries, keys, values, doc_lengths, span_order):
    kv = jnp.concatenate([keys, values], axis=1)
    kv = lax.all_gather(kv, "ctx", axis=0, tiled=True)
    local_out = attend(queries, kv, doc_lengths, span_order)
    return lax.all_to_all(local_out, "head", split_axis=0, concat_axis=1, tiled=True)


def solution(mesh):
    return jax.shard_map(
        body,
        mesh=mesh,
        in_specs=(P("ctx", "head"), P("ctx", "head"), P("ctx", "head"), P(), P()),
        out_specs=P(("ctx", "head"), None),
        check_vma=False,
    )
```

```python
import math

import jax
import jax.numpy as jnp
from jax import lax
from jax.experimental import pallas as pl
from jax.experimental.pallas import tpu as pltpu
from jax.sharding import PartitionSpec as P

HD = 128
SPAN = 128
MOST = 4096
CHUNK = 256
DEPTH = 8
MESH = pl.DeviceIdType.MESH


def doc_start(lengths_ref, ndocs, pos):
    start, end = jnp.int32(0), jnp.int32(0)
    for d in range(ndocs):
        end = end + lengths_ref[d]
        start = jnp.where(pos >= end, end, start)
    return start


def attend_kernel(
    lengths_in, order_in, q_ref, k_ref, v_ref, out_ref,
    lengths_ref, order_ref, inverse, q_st, keys, vals, top, accum, bias, sems, first_sems,
):
    small = [
        pltpu.make_async_copy(order_in, order_ref, first_sems.at[0]),
        pltpu.make_async_copy(lengths_in, lengths_ref, first_sems.at[1]),
    ]
    for copy in small:
        copy.start()
    ndocs = lengths_ref.shape[0]
    nspan = order_ref.shape[0]
    spans = q_ref.shape[0] // SPAN
    heads = q_ref.shape[1] // HD
    per = CHUNK // SPAN
    me = lax.axis_index("ctx")
    rate = math.log2(math.e) / math.sqrt(HD)

    asked = []
    for t in range(spans):
        for h in range(heads):
            copy = pltpu.make_async_copy(
                q_ref.at[t * SPAN : (t + 1) * SPAN, h * HD : (h + 1) * HD],
                q_st.at[t, h * SPAN : (h + 1) * SPAN],
                first_sems.at[2 + t * heads + h],
            )
            copy.start()
            asked.append(copy)
    for copy in small:
        copy.wait()

    @pl.loop(0, nspan)
    def _(i):
        inverse[order_ref[i]] = i

    def fetch(t, c, i):
        for j in range(per):
            slot = inverse[c * per + j]
            src = pl.ds(pl.multiple_of(slot * SPAN, SPAN), SPAN)
            dst = pl.ds(pl.multiple_of(i * CHUNK + j * SPAN, SPAN), SPAN)
            pltpu.make_async_copy(k_ref.at[src], keys.at[t, dst], sems.at[t, i, 0]).start()
            pltpu.make_async_copy(v_ref.at[src], vals.at[t, dst, :HD], sems.at[t, i, 1]).start()

    last, count, whole = [], [], []
    for t in range(spans):
        p = order_ref[me * spans + t]
        first = doc_start(lengths_ref, ndocs, p * SPAN)
        inner = doc_start(lengths_ref, ndocs, p * SPAN + SPAN - 1)
        last.append(p)
        count.append(p // per - first // CHUNK + 1)
        whole.append(inner)

        @pl.loop(0, count[t])
        def _(i):
            fetch(t, p // per - i, i)

    for t in range(spans):
        vals[t, :, HD:] = jnp.ones((vals.shape[1], HD), jnp.bfloat16)

    for copy in asked:
        copy.wait()
    for t in range(spans):
        p = last[t]
        row_pos = p * SPAN + lax.broadcasted_iota(jnp.int32, (SPAN, HD), 0)
        row_start = jnp.zeros((SPAN, HD), jnp.int32)
        end = jnp.int32(0)
        for d in range(ndocs):
            end = end + lengths_ref[d]
            row_start = jnp.where(row_pos >= end, end, row_start)

        def fold(i, masked, begin):
            rows = pl.ds(pl.multiple_of(i * CHUNK, CHUNK), CHUNK)
            if masked:
                for j in range(CHUNK // HD):
                    col = (p // per - i) * CHUNK + j * HD + lax.broadcasted_iota(
                        jnp.int32, (SPAN, HD), 1
                    )
                    ok = (col >= row_start) & (col <= row_pos)
                    bias[:, j * HD : (j + 1) * HD] = jnp.where(ok, 0.0, -1e30)
            kb = keys[t, rows]
            vb = vals[t, rows]
            for h in range(0, heads, 2):
                part = pl.ds(h * SPAN, 2 * SPAN)
                score = lax.dot_general(
                    q_st[t, part], kb, (((1,), (1,)), ((), ())),
                    preferred_element_type=jnp.float32,
                ) * rate
                if masked:
                    score = (score.reshape(2, SPAN, CHUNK) + bias[...][None]).reshape(2 * SPAN, CHUNK)
                best = jnp.max(score, axis=1, keepdims=True)
                if begin:
                    fresh = jnp.broadcast_to(best, (2 * SPAN, HD))
                else:
                    old = top[part]
                    fresh = jnp.maximum(old, best)
                weight = jnp.exp2(score - jnp.concatenate([fresh] * (CHUNK // HD), axis=1))
                made = jnp.dot(
                    weight.astype(jnp.bfloat16), vb, preferred_element_type=jnp.float32
                )
                top[part] = fresh
                if begin:
                    accum[part] = made
                else:
                    factor = jnp.exp2(old - fresh)
                    accum[part] = accum[part] * jnp.concatenate([factor, factor], axis=1) + made

        def arrive(i):
            rows = pl.ds(pl.multiple_of(i * CHUNK, CHUNK), CHUNK)
            pltpu.make_async_copy(k_ref.at[pl.ds(0, CHUNK)], keys.at[t, rows], sems.at[t, i, 0]).wait()
            pltpu.make_async_copy(v_ref.at[pl.ds(0, CHUNK)], vals.at[t, rows, :HD], sems.at[t, i, 1]).wait()

        arrive(0)
        fold(0, True, True)

        @pl.loop(1, count[t])
        def _(i):
            arrive(i)
            clear = (p // per - i) * CHUNK >= whole[t]

            @pl.when(clear)
            def _():
                fold(i, False, False)

            @pl.when(jnp.logical_not(clear))
            def _():
                fold(i, True, False)

        for h in range(heads):
            part = pl.ds(h * SPAN, SPAN)
            done = accum[part, :HD] / accum[part, HD:]
            out_ref[t * SPAN : (t + 1) * SPAN, h * HD : (h + 1) * HD] = done.astype(jnp.bfloat16)


def gather_kernel(k_in, v_in, k_out, v_out, send, recv, here):
    rows = k_in.shape[0]
    half = rows // 2
    me = lax.axis_index("ctx")
    x, z, c = me // (2 * DEPTH), (me // 2) % DEPTH, me % 2

    def block(xx, zz, cc):
        return xx * (2 * DEPTH) + ((zz + 2 * DEPTH) % DEPTH) * 2 + cc

    up, down = block(x, z + 1, c), block(x, z - 1, c)
    across, beside = block(1 - x, z, c), block(x, z, 1 - c)

    barrier = pltpu.get_barrier_semaphore()
    for other in (up, down, across, beside):
        pl.semaphore_signal(barrier, inc=1, device_id={"ctx": other}, device_id_type=MESH)
    pl.semaphore_wait(barrier, 4)

    own = pl.ds(pl.multiple_of(me * rows, rows), rows)
    stay = [
        pltpu.make_async_copy(k_in, k_out.at[own], here.at[0]),
        pltpu.make_async_copy(v_in, v_out.at[own], here.at[1]),
    ]
    for copy in stay:
        copy.start()

    sent = []

    def put(out, blk, first, count, to, kind, s, src=None):
        place = out.at[pl.ds(pl.multiple_of(blk * rows + first, half), count)]
        copy = pltpu.make_async_remote_copy(
            src_ref=place if src is None else src.at[pl.ds(first, count)],
            dst_ref=place,
            send_sem=send.at[kind, s],
            recv_sem=recv.at[kind, s],
            device_id={"ctx": to},
            device_id_type=MESH,
        )
        copy.start()
        sent.append(copy)

    def got(out, blk, first, count, kind, s):
        place = out.at[pl.ds(pl.multiple_of(blk * rows + first, half), count)]
        pltpu.make_async_remote_copy(
            src_ref=place,
            dst_ref=place,
            send_sem=send.at[kind, s],
            recv_sem=recv.at[kind, s],
            device_id={"ctx": beside},
            device_id_type=MESH,
        ).wait_recv()

    ways = ((k_out, k_in, up, -1, 0), (v_out, v_in, down, 1, 1))
    for out, src, to, sign, i in ways:
        put(out, me, 0, half, across, 6 + i, 0, src)
        put(out, me, 0, rows, to, 0 + i, 0, src)
    for out, src, to, sign, i in ways:
        put(out, me, half, half, across, 4 + i, 0, src)
        put(out, me, 0, rows, beside, 8 + i, 0, src)
    for out, src, to, sign, i in ways:
        blk = block(1 - x, z, c)
        got(out, blk, 0, half, 6 + i, 0)
        put(out, blk, 0, half, to, 2 + i, 0)
        put(out, blk, 0, half, beside, 10 + i, 0)
    for s in range(1, DEPTH):
        for out, src, to, sign, i in ways:
            blk = block(x, z + sign * s, c)
            got(out, blk, 0, rows, 0 + i, s - 1)
            if s < DEPTH - 1:
                put(out, blk, 0, rows, to, 0 + i, s)
            put(out, blk, half, half, across, 4 + i, s)
            put(out, blk, 0, rows, beside, 8 + i, s)
        for out, src, to, sign, i in ways:
            blk = block(1 - x, z + sign * s, c)
            got(out, blk, 0, half, 2 + i, s - 1)
            if s < DEPTH - 1:
                put(out, blk, 0, half, to, 2 + i, s)
            put(out, blk, 0, half, beside, 10 + i, s)
        for out, src, to, sign, i in ways:
            blk = block(1 - x, z + sign * (s - 1), c)
            got(out, blk, half, half, 4 + i, s - 1)
            put(out, blk, half, half, beside, 12 + i, s - 1)
    for out, src, to, sign, i in ways:
        blk = block(1 - x, z + sign * (DEPTH - 1), c)
        got(out, blk, half, half, 4 + i, DEPTH - 1)
        put(out, blk, half, half, beside, 12 + i, DEPTH - 1)
    for s in range(DEPTH):
        for out, src, to, sign, i in ways:
            got(out, block(x, z + sign * s, 1 - c), 0, rows, 8 + i, s)
            got(out, block(1 - x, z + sign * s, 1 - c), 0, half, 10 + i, s)
            got(out, block(1 - x, z + sign * s, 1 - c), half, half, 12 + i, s)
    for copy in sent:
        copy.wait_send()
    for copy in stay:
        copy.wait()


def gather(keys, values):
    rows, width = keys.shape
    whole = jax.ShapeDtypeStruct((rows * lax.axis_size("ctx"), width), keys.dtype)
    return pl.pallas_call(
        gather_kernel,
        out_shape=(whole, whole),
        in_specs=[pl.BlockSpec(memory_space=pltpu.HBM)] * 2,
        out_specs=(pl.BlockSpec(memory_space=pltpu.HBM),) * 2,
        scratch_shapes=[
            pltpu.SemaphoreType.DMA((14, DEPTH)),
            pltpu.SemaphoreType.DMA((14, DEPTH)),
            pltpu.SemaphoreType.DMA((2,)),
        ],
        compiler_params=pltpu.CompilerParams(collective_id=0, has_side_effects=True),
        name="gather",
    )(keys, values)


def attend(queries, keys, values, doc_lengths, span_order):
    rows, width = queries.shape
    heads, spans = width // HD, rows // SPAN
    chunks = MOST // CHUNK + 1
    hbm = pl.BlockSpec(memory_space=pltpu.HBM)
    return pl.pallas_call(
        attend_kernel,
        out_shape=jax.ShapeDtypeStruct((rows, width), jnp.bfloat16),
        in_specs=[hbm] * 5,
        out_specs=pl.BlockSpec(memory_space=pltpu.VMEM),
        scratch_shapes=[
            pltpu.SMEM(doc_lengths.shape, jnp.int32),
            pltpu.SMEM(span_order.shape, jnp.int32),
            pltpu.SMEM((span_order.shape[0],), jnp.int32),
            pltpu.VMEM((spans, heads * SPAN, HD), jnp.bfloat16),
            pltpu.VMEM((spans, chunks * CHUNK, HD), jnp.bfloat16),
            pltpu.VMEM((spans, chunks * CHUNK, 2 * HD), jnp.bfloat16),
            pltpu.VMEM((heads * SPAN, HD), jnp.float32),
            pltpu.VMEM((heads * SPAN, 2 * HD), jnp.float32),
            pltpu.VMEM((SPAN, CHUNK), jnp.float32),
            pltpu.SemaphoreType.DMA((spans, chunks, 2)),
            pltpu.SemaphoreType.DMA((2 + spans * heads,)),
        ],
        compiler_params=pltpu.CompilerParams(vmem_limit_bytes=40 * 2**20),
        name="attend",
    )(doc_lengths, span_order, queries, keys, values)


def body(queries, keys, values, doc_lengths, span_order):
    keys, values = gather(keys, values)
    local_out = attend(queries, keys, values, doc_lengths, span_order)
    return lax.all_to_all(local_out, "head", split_axis=0, concat_axis=1, tiled=True)


def solution(mesh):
    return jax.shard_map(
        body,
        mesh=mesh,
        in_specs=(P("ctx", "head"), P("ctx", "head"), P("ctx", "head"), P(), P()),
        out_specs=P(("ctx", "head"), None),
        check_vma=False,
    )
```

```python
import math

import jax
import jax.numpy as jnp
from jax import lax
from jax.experimental import pallas as pl
from jax.experimental.pallas import tpu as pltpu
from jax.sharding import PartitionSpec as P

HD = 128
SPAN = 128
DEPTH = 8
CHUNK = 512
NCHUNK = 16
FAR = -(2.0**100)
RATE = math.log2(math.e) / math.sqrt(HD)
MESH = pl.DeviceIdType.MESH
RING, CROSS, BESIDE = 0, 24, 36
KIND = {"V": 0, "K": 1, "P": 2}


def kernel(
    lengths_ref, order_ref, q_ref, k_in, v_in, out_ref,
    buf, qa, acc, top, ka, va, s0, s1, row_pos, row_start, o_st,
    send, recv, o_send, o_recv, here, q_sem,
):
    rows = k_in.shape[0]
    spans = rows // SPAN
    heads = q_ref.shape[1] // HD
    group = heads * SPAN
    width = q_ref.shape[1]
    nheads = lax.axis_size("head")
    share = rows // nheads
    ndocs = lengths_ref.shape[0]
    me = lax.axis_index("ctx")
    my_head = lax.axis_index("head")
    x, z, c = me // (2 * DEPTH), (me // 2) % DEPTH, me % 2
    sign = 1 - 2 * c

    def block(px, dz, flip):
        xx = x + px - 2 * x * px
        cc = c + flip - 2 * c * flip
        return xx * (2 * DEPTH) + ((z + dz + 2 * DEPTH) % DEPTH) * 2 + cc

    up, down, across, beside = block(0, 1, 0), block(0, -1, 0), block(1, 0, 0), block(0, 0, 1)
    far_to, far_from = block(0, sign, 0), {0: block(0, -3 * sign, 0), 1: block(1, -3 * sign, 0)}
    near = {
        (px, dz, f): block(px, dz, f) for px in (0, 1) for dz in range(-3, 5) for f in (0, 1)
    }

    barrier = pltpu.get_barrier_semaphore()
    for other in (up, down, across, beside):
        pl.semaphore_signal(barrier, inc=1, device_id={"ctx": other}, device_id_type=MESH)
    for j in range(1, nheads):
        pl.semaphore_signal(
            barrier, inc=1, device_id={"head": lax.rem(my_head + j, nheads)}, device_id_type=MESH
        )

    K, V, KV = (0, rows), (rows, rows), (0, 2 * rows)
    PART = {"V": V, "K": K, "P": K}
    PX = {"V": 0, "K": 0, "P": 1}

    def place(blk, part):
        return buf.at[pl.ds(pl.multiple_of(blk * (2 * rows) + part[0], rows), part[1])]

    stay = [
        pltpu.make_async_copy(k_in, place(me, K), here.at[0]),
        pltpu.make_async_copy(v_in, place(me, V), here.at[1]),
    ]
    asked = []
    for t in range(spans):
        for h in range(heads):
            asked.append(
                pltpu.make_async_copy(
                    q_ref.at[t * SPAN : (t + 1) * SPAN, h * HD : (h + 1) * HD],
                    qa.at[t * group + h * SPAN : t * group + (h + 1) * SPAN, 0:HD],
                    q_sem.at[t * heads + h],
                )
            )
    for copy in stay + asked:
        copy.start()

    sent = {}

    def put(blk, part, to, sem, src=None):
        place_there = place(blk, part)
        pltpu.make_async_remote_copy(
            src_ref=place_there if src is None else src,
            dst_ref=place_there,
            send_sem=send.at[sem],
            recv_sem=recv.at[sem],
            device_id={"ctx": to},
            device_id_type=MESH,
        ).start()
        sent[sem] = part

    def mirror(blk, part, sem):
        spot = place(blk, part)
        return pltpu.make_async_remote_copy(
            src_ref=spot,
            dst_ref=spot,
            send_sem=send.at[sem],
            recv_sem=recv.at[sem],
            device_id={"ctx": beside},
            device_id_type=MESH,
        )

    def got(blk, part, sem):
        mirror(blk, part, sem).wait_recv()

    ways = ((0, up, 1), (1, down, -1))

    def ring(kind, s, way):
        return RING + (s - 1) * 6 + KIND[kind] * 2 + way

    def step_of(s, way):
        return 1 + (s - 1) * 2 + way

    def onward(kind, s):
        for way, to, d in ways:
            blk = near[PX[kind], -d * s, 0]
            got(blk, PART[kind], ring(kind, s, way))
            if s < 3:
                put(blk, PART[kind], to, ring(kind, s + 1, way))
            if kind == "V":
                put(blk, V, across, CROSS + 1 + step_of(s, way))
        if s == 3:
            put(far_from[PX[kind]], PART[kind], far_to, ring(kind, 4, 0))
        for way, to, d in ways:
            blk = near[PX[kind], -d * s, 0]
            if kind == "K":
                put(blk, KV, beside, BESIDE + step_of(s, way))
            if kind == "P":
                put(blk, K, beside, BESIDE + 8 + step_of(s, way))

    def crossed(s):
        for way, to, d in ways:
            blk = near[1, -d * s, 0]
            got(blk, V, CROSS + 1 + step_of(s, way))
            put(blk, V, beside, BESIDE + 16 + step_of(s, way))

    def last(kind):
        blk = near[PX[kind], 4, 0]
        got(blk, PART[kind], ring(kind, 4, 0))
        if kind == "V":
            put(blk, V, across, CROSS + 8)
        if kind == "K":
            put(blk, KV, beside, BESIDE + 7)
        if kind == "P":
            put(blk, K, beside, BESIDE + 8 + 7)

    def crossed_last():
        got(near[1, 4, 0], V, CROSS + 8)
        put(near[1, 4, 0], V, beside, BESIDE + 16 + 7)

    def crossed_first():
        got(near[1, 0, 0], V, CROSS + 1)
        put(near[1, 0, 0], V, beside, BESIDE + 16)

    def need_own(s):
        for way, to, d in ways:
            got(near[0, -d * s, 1], KV, BESIDE + step_of(s, way))

    def need_other(s):
        for way, to, d in ways:
            got(near[1, -d * s, 1], K, BESIDE + 8 + step_of(s, way))
            got(near[1, -d * s, 1], V, BESIDE + 16 + step_of(s, way))

    def need_first():
        got(near[1, 0, 1], K, BESIDE + 8)
        got(near[1, 0, 1], V, BESIDE + 16)

    def need_last():
        got(near[0, 4, 1], KV, BESIDE + 7)
        got(near[1, 4, 1], K, BESIDE + 8 + 7)
        got(near[1, 4, 1], V, BESIDE + 16 + 7)

    middle = {
        0: [crossed_first, need_first],
        1: [lambda: onward("K", 1)],
        2: [lambda: need_own(1)],
        3: [lambda: onward("V", 2)],
        4: [lambda: need_other(1)],
        5: [lambda: crossed(2)],
        6: [lambda: need_own(2), lambda: onward("K", 3)],
        7: [lambda: crossed(3)],
        8: [lambda: need_other(2), lambda: last("K")],
        10: [lambda: need_own(3)],
    }
    finish = {
        0: [lambda: onward("V", 1)],
        1: [lambda: onward("P", 1)],
        2: [lambda: crossed(1)],
        3: [lambda: onward("K", 2)],
        4: [lambda: onward("P", 2)],
        5: [lambda: onward("V", 3)],
        6: [lambda: onward("P", 3)],
        7: [lambda: last("V")],
        8: [lambda: last("P")],
        9: [crossed_last],
        11: [lambda: need_other(3)],
        12: [need_last],
    }

    def chunk_blocks(m):
        s, k = (m + 2) // 4, (m + 2) % 4
        e0, e4 = 1 - (s + 3) // 4, s // 4
        mid = 1 - e0 - e4
        low, high = k % 2, k // 2
        flip = (1 - e0) * low
        return (
            block(e0 * low + mid * high, -s, flip),
            block(e0 * low + e4 + mid * high, s, e0 + flip),
        )

    def prepare(m):
        slot = m % 4
        for j, blk in enumerate(chunk_blocks(m)):
            base = pl.multiple_of(blk * (2 * rows), 2 * rows)
            va[pl.ds(pl.multiple_of(slot * CHUNK + j * rows, rows), rows), 0:HD] = buf[
                pl.ds(base + rows, rows)
            ]
            keys = buf[pl.ds(base, rows)]
            for t in range(spans):
                first = pl.multiple_of((slot * spans + t) * CHUNK + j * rows, rows)
                ka[pl.ds(first, rows), 0:HD] = keys
                for i in range(spans):
                    pos = order_ref[blk * spans + i] * SPAN + lax.broadcasted_iota(
                        jnp.int32, (SPAN, SPAN), 0
                    )
                    ok = (pos >= row_start[t, 0:1]) & (pos <= row_pos[t, 0:1])
                    ka[pl.ds(first + i * SPAN, SPAN), HD:] = jnp.where(ok, 0.0, FAR).astype(
                        jnp.bfloat16
                    )

    def scores(m, t, dest):
        first = pl.multiple_of(((m % 4) * spans + t) * CHUNK, CHUNK)
        dest[...] = lax.dot_general(
            qa[pl.ds(pl.multiple_of(t * group, group), group)],
            ka[pl.ds(first, CHUNK)],
            (((1,), (1,)), ((), ())),
            preferred_element_type=jnp.float32,
        )

    def fold(m, t, source):
        part = pl.ds(pl.multiple_of(t * group, group), group)
        score = source[...]
        old = top[part]
        new = jnp.maximum(old, jnp.max(score, axis=1, keepdims=True))
        weight = jnp.exp2((score - jnp.concatenate([new] * (CHUNK // HD), axis=1)) * RATE)
        factor = jnp.exp2((old - new) * RATE)
        made = jnp.dot(
            weight.astype(jnp.bfloat16),
            va[pl.ds(pl.multiple_of((m % 4) * CHUNK, CHUNK), CHUNK)],
            preferred_element_type=jnp.float32,
        )
        top[part] = new
        acc[part] = acc[part] * jnp.concatenate([factor, factor], axis=1) + made

    def hand_out(t):
        for h in range(heads):
            part = slice(t * group + h * SPAN, t * group + (h + 1) * SPAN)
            done = acc[part, 0:HD] / acc[part, HD:]
            o_st[t * SPAN : (t + 1) * SPAN, h * HD : (h + 1) * HD] = done.astype(jnp.bfloat16)
        columns = pl.ds(pl.multiple_of(my_head * width, width), width)
        for r in range(SPAN // share):
            j = t * (SPAN // share) + r
            source = o_st.at[j * share : (j + 1) * share]

            @pl.when(my_head != j)
            def _():
                pltpu.make_async_remote_copy(
                    src_ref=source,
                    dst_ref=out_ref.at[:, columns],
                    send_sem=o_send.at[j],
                    recv_sem=o_recv.at[my_head],
                    device_id={"head": j},
                    device_id_type=MESH,
                ).start()

            @pl.when(my_head == j)
            def _():
                pltpu.make_async_copy(source, out_ref.at[:, columns], here.at[2]).start()

    pl.semaphore_wait(barrier, 4 + nheads - 1)
    put(me, K, across, CROSS + 0, k_in)
    for way, to, d in ways:
        put(me, V, to, ring("V", 1, way), v_in)
    put(me, V, across, CROSS + 1, v_in)
    for way, to, d in ways:
        put(me, K, to, ring("K", 1, way), k_in)
    for copy in stay:
        copy.wait()
    put(me, KV, beside, BESIDE + 0)

    eye = (
        lax.broadcasted_iota(jnp.int32, (SPAN, SPAN), 0)
        == lax.broadcasted_iota(jnp.int32, (SPAN, SPAN), 1)
    ).astype(jnp.bfloat16)
    for t in range(spans):
        pos = order_ref[me * spans + t] * SPAN + lax.broadcasted_iota(jnp.int32, (8, SPAN), 1)
        start, end = jnp.zeros((8, SPAN), jnp.int32), jnp.int32(0)
        for d in range(ndocs):
            end = end + lengths_ref[d]
            start = jnp.where(pos >= end, end, start)
        row_pos[t], row_start[t] = pos, start
        for h in range(heads):
            qa[t * group + h * SPAN : t * group + (h + 1) * SPAN, HD:] = eye
    va[:, HD:] = jnp.ones((va.shape[0], HD), jnp.bfloat16)
    acc[...] = jnp.zeros_like(acc)
    top[...] = jnp.full(top.shape, -1e30, jnp.float32)
    for copy in asked:
        copy.wait()

    got(near[1, 0, 0], K, CROSS + 0)
    for way, to, d in ways:
        put(near[1, 0, 0], K, to, ring("P", 1, way))
    put(near[1, 0, 0], K, beside, BESIDE + 8)
    got(near[0, 0, 1], KV, BESIDE + 0)
    prepare(0)
    scores(0, 0, s0)

    @pl.loop(0, NCHUNK)
    def _(u):
        tail = u // 12
        v = (u - 12) * tail
        t_a = tail * (v // 2)
        t_b = 1 - tail + t_a
        m_a = (1 - tail) * u + tail * (12 + 2 * (v % 2))
        m_b = m_a + tail
        nxt = v + 1
        early = (1 - tail) * (u + 1)
        t_n = tail * ((nxt // 2) % 2)
        m_n = early + tail * (12 + 2 * (nxt % 2))
        m_p = early + tail * (14 + (v + 2) // 3)
        scores(m_b, t_b, s1)
        fold(m_a, t_a, s0)
        for key, jobs in middle.items():

            @pl.when(u == key)
            def _(jobs=jobs):
                for job in jobs:
                    job()

        @pl.when(u < 13)
        def _():
            prepare(m_p)

        scores(m_n, t_n, s0)
        fold(m_b, t_b, s1)
        for key, jobs in finish.items():

            @pl.when(u == key)
            def _(jobs=jobs):
                for job in jobs:
                    job()

        @pl.when(u == 11)
        def _():
            prepare(13)

        @pl.when(u == 12)
        def _():
            prepare(15)

        @pl.when(u == 13)
        def _():
            hand_out(0)

    hand_out(1)
    for sem, part in sent.items():
        mirror(me, part, sem).wait_send()

    columns = pl.ds(pl.multiple_of(my_head * width, width), width)
    for j in range(nheads):
        source = o_st.at[j * share : (j + 1) * share]
        landing = pltpu.make_async_remote_copy(
            src_ref=source,
            dst_ref=out_ref.at[:, j * width : (j + 1) * width],
            send_sem=o_send.at[j],
            recv_sem=o_recv.at[j],
            device_id={"head": j},
            device_id_type=MESH,
        )

        @pl.when(my_head != j)
        def _():
            landing.wait_recv()
            landing.wait_send()

        @pl.when(my_head == j)
        def _():
            pltpu.make_async_copy(source, out_ref.at[:, columns], here.at[2]).wait()


def body(queries, keys, values, doc_lengths, span_order):
    rows, width = queries.shape
    heads, spans = width // HD, rows // SPAN
    n_ctx, nheads = lax.axis_size("ctx"), lax.axis_size("head")
    group = heads * SPAN
    smem, hbm = pl.BlockSpec(memory_space=pltpu.SMEM), pl.BlockSpec(memory_space=pltpu.HBM)
    f32, bf16, i32 = jnp.float32, jnp.bfloat16, jnp.int32
    return pl.pallas_call(
        kernel,
        out_shape=jax.ShapeDtypeStruct((rows // nheads, width * nheads), bf16),
        in_specs=[smem, smem, hbm, hbm, hbm],
        out_specs=hbm,
        scratch_shapes=[
            pltpu.VMEM((n_ctx * 2 * rows, HD), bf16),
            pltpu.VMEM((spans * group, 2 * HD), bf16),
            pltpu.VMEM((spans * group, 2 * HD), f32),
            pltpu.VMEM((spans * group, HD), f32),
            pltpu.VMEM((4 * spans * CHUNK, 2 * HD), bf16),
            pltpu.VMEM((4 * CHUNK, 2 * HD), bf16),
            pltpu.VMEM((group, CHUNK), f32),
            pltpu.VMEM((group, CHUNK), f32),
            pltpu.VMEM((spans, 8, SPAN), i32),
            pltpu.VMEM((spans, 8, SPAN), i32),
            pltpu.VMEM((rows, width), bf16),
            pltpu.SemaphoreType.DMA((60,)),
            pltpu.SemaphoreType.DMA((60,)),
            pltpu.SemaphoreType.DMA((nheads,)),
            pltpu.SemaphoreType.DMA((nheads,)),
            pltpu.SemaphoreType.DMA((3,)),
            pltpu.SemaphoreType.DMA((spans * heads,)),
        ],
        compiler_params=pltpu.CompilerParams(
            collective_id=0, has_side_effects=True, vmem_limit_bytes=60 * 2**20
        ),
        name="attend",
    )(doc_lengths, span_order, queries, keys, values)


def solution(mesh):
    return jax.shard_map(
        body,
        mesh=mesh,
        in_specs=(P("ctx", "head"), P("ctx", "head"), P("ctx", "head"), P(), P()),
        out_specs=P(("ctx", "head"), None),
        check_vma=False,
    )
```

```python
import math

import jax
import jax.numpy as jnp
from jax import lax
from jax.experimental import pallas as pl
from jax.experimental.pallas import tpu as pltpu
from jax.sharding import PartitionSpec as P

HD = 128
SPAN = 128
DEPTH = 8
CHUNK = 512
NCHUNK = 16
FAR = -(2.0**100)
RATE = math.log2(math.e) / math.sqrt(HD)
MESH = pl.DeviceIdType.MESH
VALS, KEYS, GUEST, FIRST, OVER, SIDE = 0, 7, 14, 21, 23, 30


def _pair(p, s, flip):
    return ((p, -s, flip), (p, s, flip))


ORDER = (
    ((0, 0, 0), (0, 0, 1)), _pair(0, 1, 0), ((1, 0, 0), (1, 0, 1)), _pair(0, 1, 1),
    _pair(0, 2, 0), _pair(1, 1, 0), _pair(0, 2, 1), _pair(1, 1, 1),
    _pair(0, 3, 0), _pair(1, 2, 0), _pair(0, 3, 1), _pair(1, 2, 1),
    _pair(1, 3, 0), _pair(1, 3, 1), ((0, 4, 0), (1, 4, 0)), ((0, 4, 1), (1, 4, 1)),
)


def kernel(
    lengths_ref, order_ref, q_ref, k_in, v_in, out_ref,
    buf, qa, acc, top, bias, s0, s1, row_pos, row_start, o_st,
    send, recv, o_send, o_recv, here, q_sem,
):
    rows = k_in.shape[0]
    spans = rows // SPAN
    heads = q_ref.shape[1] // HD
    group = heads * SPAN
    width = q_ref.shape[1]
    nheads = lax.axis_size("head")
    n_ctx = lax.axis_size("ctx")
    share = rows // nheads
    ndocs = lengths_ref.shape[0]
    me = lax.axis_index("ctx")
    my_head = lax.axis_index("head")
    x, z, c = me // (2 * DEPTH), (me // 2) % DEPTH, me % 2
    sign = 1 - 2 * c

    def block(px, dz, flip):
        xx = x + px - 2 * x * px
        cc = c + flip - 2 * c * flip
        return xx * (2 * DEPTH) + ((z + dz + 2 * DEPTH) % DEPTH) * 2 + cc

    across, beside = block(1, 0, 0), block(0, 0, 1)
    hop = {0: block(0, 1, 0), 1: block(0, -1, 0)}
    far_to, far_from = block(0, sign, 0), {p: block(p, -3 * sign, 0) for p in (0, 1)}
    near = {
        (px, dz, f): block(px, dz, f) for px in (0, 1) for dz in range(-3, 5) for f in (0, 1)
    }

    barrier = pltpu.get_barrier_semaphore()
    for other in (*hop.values(), across, beside):
        pl.semaphore_signal(barrier, inc=1, device_id={"ctx": other}, device_id_type=MESH)
    for j in range(1, nheads):
        pl.semaphore_signal(
            barrier, inc=1, device_id={"head": lax.rem(my_head + j, nheads)}, device_id_type=MESH
        )

    K, V, KV = (0, rows), (rows, rows), (0, 2 * rows)

    def place(blk, part):
        return buf.at[pl.ds(pl.multiple_of(blk * (2 * rows) + part[0], rows), part[1])]

    stay = [
        pltpu.make_async_copy(k_in, place(me, K), here.at[0]),
        pltpu.make_async_copy(v_in, place(me, V), here.at[1]),
    ]
    asked = []
    for t in range(spans):
        for h in range(heads):
            asked.append(
                pltpu.make_async_copy(
                    q_ref.at[t * SPAN : (t + 1) * SPAN, h * HD : (h + 1) * HD],
                    qa.at[t * group + h * SPAN : t * group + (h + 1) * SPAN, 0:HD],
                    q_sem.at[t * heads + h],
                )
            )
    for copy in stay + asked:
        copy.start()

    sent = {}

    def put(blk, part, to, sem):
        place_there = place(blk, part)
        pltpu.make_async_remote_copy(
            src_ref=place_there,
            dst_ref=place_there,
            send_sem=send.at[sem],
            recv_sem=recv.at[sem],
            device_id={"ctx": to},
            device_id_type=MESH,
        ).start()
        sent[sem] = part

    def mirror(blk, part, sem):
        spot = place(blk, part)
        return pltpu.make_async_remote_copy(
            src_ref=spot,
            dst_ref=spot,
            send_sem=send.at[sem],
            recv_sem=recv.at[sem],
            device_id={"ctx": beside},
            device_id_type=MESH,
        )

    def got(blk, part, sem):
        mirror(blk, part, sem).wait_recv()

    ways = ((0, 1), (1, -1))

    def of(first, s, way):
        return first + (s - 1) * 2 + way

    RIDES = {"V": (0, V, VALS), "K": (0, K, KEYS), "P": (1, K, GUEST)}

    def ride(kind, s):
        p, part, first = RIDES[kind]
        if s == 4:
            got(near[p, 4, 0], part, first + 6)
            if kind == "V":
                put(near[0, 4, 0], V, across, OVER + 6)
            return
        for w, d in ways:
            blk = near[p, -s * d, 0]
            got(blk, part, of(first, s, w))
            if s < 3:
                put(blk, part, hop[w], of(first, s + 1, w))
        if s == 3:
            put(far_from[p], part, far_to, first + 6)
        if kind == "V":
            for w, d in ways:
                put(near[0, -s * d, 0], V, across, of(OVER, s, w))

    def pass_own(s):
        if s == 4:
            put(near[0, 4, 0], KV, beside, SIDE + 7)
            return
        for w, d in ways:
            put(near[0, -s * d, 0], KV, beside, SIDE + of(1, s, w))

    def guest_0():
        got(near[1, 0, 0], K, FIRST)
        for w, d in ways:
            put(near[1, 0, 0], K, hop[w], of(GUEST, 1, w))

    def other(s):
        if s == 0:
            got(near[1, 0, 0], V, FIRST + 1)
            put(near[1, 0, 0], KV, beside, SIDE + 8)
        elif s == 4:
            got(near[1, 4, 0], V, OVER + 6)
            put(near[1, 4, 0], KV, beside, SIDE + 8 + 7)
        else:
            for w, d in ways:
                blk = near[1, -s * d, 0]
                got(blk, V, of(OVER, s, w))
                put(blk, KV, beside, SIDE + 8 + of(1, s, w))

    def side(p, s):
        if s == 0:
            got(near[p, 0, 1], KV, SIDE + 8 * p)
        elif s == 4:
            got(near[p, 4, 1], KV, SIDE + 8 * p + 7)
        else:
            for w, d in ways:
                got(near[p, -d * s, 1], KV, SIDE + 8 * p + of(1, s, w))

    middle = {
        0: [guest_0, lambda: ride("V", 1), lambda: other(0), lambda: ride("K", 1), lambda: pass_own(1)],
        1: [lambda: side(1, 0)],
        2: [lambda: side(0, 1)],
        3: [lambda: ride("K", 2), lambda: pass_own(2)],
        5: [lambda: side(0, 2)],
        6: [lambda: ride("P", 3), lambda: side(1, 1)],
        7: [lambda: ride("K", 4), lambda: pass_own(4)],
        9: [lambda: ride("P", 4), lambda: other(4), lambda: side(0, 3)],
        10: [lambda: side(1, 2)],
    }
    finish = {
        1: [lambda: ride("P", 1)],
        2: [lambda: ride("V", 2), lambda: other(1)],
        3: [lambda: ride("P", 2)],
        4: [lambda: ride("V", 3)],
        5: [lambda: ride("K", 3), lambda: other(2), lambda: pass_own(3)],
        6: [lambda: ride("V", 4)],
        7: [lambda: other(3)],
        11: [lambda: side(1, 3)],
        12: [lambda: side(0, 4), lambda: side(1, 4)],
    }

    def chunk_blocks(m):
        def digit(code):
            return lax.rem(lax.shift_right_logical(jnp.int32(code), m), 2)

        found = []
        for i in range(2):
            px, far, flip = ([ORDER[n][i][f] for n in range(NCHUNK)] for f in range(3))
            dz = sum(
                (1 << e) * digit(sum(((v % DEPTH) >> e & 1) << n for n, v in enumerate(far)))
                for e in range(3)
            )
            code = [sum(v << n for n, v in enumerate(row)) for row in (px, flip)]
            found.append(block(digit(code[0]), dz, digit(code[1])))
        return found

    def keys_of(m, t):
        parts = []
        for blk in chunk_blocks(m):
            base = pl.multiple_of(blk * (2 * rows), 2 * rows)
            hide = pl.multiple_of(t * (rows * n_ctx) + blk * rows, rows)
            parts.append(jnp.concatenate([buf[pl.ds(base, rows)], bias[pl.ds(hide, rows)]], axis=1))
        return jnp.concatenate(parts, axis=0)

    def values_of(m):
        parts = []
        for blk in chunk_blocks(m):
            base = pl.multiple_of(blk * (2 * rows) + rows, rows)
            parts.append(
                jnp.concatenate([buf[pl.ds(base, rows)], jnp.ones((rows, HD), jnp.bfloat16)], axis=1)
            )
        return jnp.concatenate(parts, axis=0)

    def scores(m, t, dest):
        dest[...] = lax.dot_general(
            qa[pl.ds(pl.multiple_of(t * group, group), group)],
            keys_of(m, t),
            (((1,), (1,)), ((), ())),
            preferred_element_type=jnp.float32,
        )

    def fold(m, t, source):
        part = pl.ds(pl.multiple_of(t * group, group), group)
        score = source[...]
        old = top[part]
        new = jnp.maximum(old, jnp.max(score, axis=1, keepdims=True))
        weight = jnp.exp2((score - jnp.concatenate([new] * (CHUNK // HD), axis=1)) * RATE)
        factor = jnp.exp2((old - new) * RATE)
        made = jnp.dot(
            weight.astype(jnp.bfloat16), values_of(m), preferred_element_type=jnp.float32
        )
        top[part] = new
        acc[part] = acc[part] * jnp.concatenate([factor, factor], axis=1) + made

    def hand_out(t):
        for h in range(heads):
            part = slice(t * group + h * SPAN, t * group + (h + 1) * SPAN)
            done = acc[part, 0:HD] / acc[part, HD:]
            o_st[t * SPAN : (t + 1) * SPAN, h * HD : (h + 1) * HD] = done.astype(jnp.bfloat16)
        columns = pl.ds(pl.multiple_of(my_head * width, width), width)
        for r in range(SPAN // share):
            j = t * (SPAN // share) + r
            source = o_st.at[j * share : (j + 1) * share]

            @pl.when(my_head != j)
            def _():
                pltpu.make_async_remote_copy(
                    src_ref=source,
                    dst_ref=out_ref.at[:, columns],
                    send_sem=o_send.at[j],
                    recv_sem=o_recv.at[my_head],
                    device_id={"head": j},
                    device_id_type=MESH,
                ).start()

            @pl.when(my_head == j)
            def _():
                pltpu.make_async_copy(source, out_ref.at[:, columns], here.at[2]).start()

    eye = (
        lax.broadcasted_iota(jnp.int32, (SPAN, SPAN), 0)
        == lax.broadcasted_iota(jnp.int32, (SPAN, SPAN), 1)
    ).astype(jnp.bfloat16)
    for t in range(spans):
        pos = order_ref[me * spans + t] * SPAN + lax.broadcasted_iota(jnp.int32, (8, SPAN), 1)
        start, end = jnp.zeros((8, SPAN), jnp.int32), jnp.int32(0)
        for d in range(ndocs):
            end = end + lengths_ref[d]
            start = jnp.where(pos >= end, end, start)
        row_pos[t], row_start[t] = pos, start
        for h in range(heads):
            qa[t * group + h * SPAN : t * group + (h + 1) * SPAN, HD:] = eye
    acc[...] = jnp.zeros_like(acc)
    top[...] = jnp.full(top.shape, -1e30, jnp.float32)

    pl.semaphore_wait(barrier, 4 + nheads - 1)
    for copy in stay:
        copy.wait()
    put(me, K, across, FIRST)
    for w, d in ways:
        put(me, V, hop[w], of(VALS, 1, w))
    put(me, V, across, FIRST + 1)
    for w, d in ways:
        put(me, K, hop[w], of(KEYS, 1, w))
    put(me, KV, beside, SIDE)

    @pl.loop(0, n_ctx * spans, unroll=4)
    def _(i):
        pos = order_ref[i] * SPAN + lax.broadcasted_iota(jnp.int32, (SPAN, SPAN), 0)
        for t in range(spans):
            ok = (pos >= row_start[t, 0:1]) & (pos <= row_pos[t, 0:1])
            spot = pl.multiple_of(t * (rows * n_ctx) + i * SPAN, SPAN)
            bias[pl.ds(spot, SPAN)] = jnp.where(ok, 0.0, FAR).astype(jnp.bfloat16)

    for copy in asked:
        copy.wait()

    side(0, 0)
    scores(0, 0, s0)

    @pl.loop(0, NCHUNK)
    def _(u):
        tail = u // 12
        v = (u - 12) * tail
        t_a = tail * (v // 2)
        t_b = 1 - tail + t_a
        m_a = (1 - tail) * u + tail * (12 + 2 * (v % 2))
        m_b = m_a + tail
        nxt = v + 1
        early = (1 - tail) * (u + 1)
        t_n = tail * ((nxt // 2) % 2)
        m_n = early + tail * (12 + 2 * (nxt % 2))
        scores(m_b, t_b, s1)
        fold(m_a, t_a, s0)
        for key, jobs in middle.items():

            @pl.when(u == key)
            def _(jobs=jobs):
                for job in jobs:
                    job()

        scores(m_n, t_n, s0)
        fold(m_b, t_b, s1)
        for key, jobs in finish.items():

            @pl.when(u == key)
            def _(jobs=jobs):
                for job in jobs:
                    job()

        @pl.when(u == 13)
        def _():
            hand_out(0)

    hand_out(1)
    for sem, part in sent.items():
        mirror(me, part, sem).wait_send()

    columns = pl.ds(pl.multiple_of(my_head * width, width), width)
    for j in range(nheads):
        source = o_st.at[j * share : (j + 1) * share]
        landing = pltpu.make_async_remote_copy(
            src_ref=source,
            dst_ref=out_ref.at[:, j * width : (j + 1) * width],
            send_sem=o_send.at[j],
            recv_sem=o_recv.at[j],
            device_id={"head": j},
            device_id_type=MESH,
        )

        @pl.when(my_head != j)
        def _():
            landing.wait_recv()
            landing.wait_send()

        @pl.when(my_head == j)
        def _():
            pltpu.make_async_copy(source, out_ref.at[:, columns], here.at[2]).wait()


def body(queries, keys, values, doc_lengths, span_order):
    rows, width = queries.shape
    heads, spans = width // HD, rows // SPAN
    n_ctx, nheads = lax.axis_size("ctx"), lax.axis_size("head")
    group = heads * SPAN
    smem, hbm = pl.BlockSpec(memory_space=pltpu.SMEM), pl.BlockSpec(memory_space=pltpu.HBM)
    f32, bf16, i32 = jnp.float32, jnp.bfloat16, jnp.int32
    return pl.pallas_call(
        kernel,
        out_shape=jax.ShapeDtypeStruct((rows // nheads, width * nheads), bf16),
        in_specs=[smem, smem, hbm, hbm, hbm],
        out_specs=hbm,
        scratch_shapes=[
            pltpu.VMEM((n_ctx * 2 * rows, HD), bf16),
            pltpu.VMEM((spans * group, 2 * HD), bf16),
            pltpu.VMEM((spans * group, 2 * HD), f32),
            pltpu.VMEM((spans * group, HD), f32),
            pltpu.VMEM((spans * n_ctx * rows, HD), bf16),
            pltpu.VMEM((group, CHUNK), f32),
            pltpu.VMEM((group, CHUNK), f32),
            pltpu.VMEM((spans, 8, SPAN), i32),
            pltpu.VMEM((spans, 8, SPAN), i32),
            pltpu.VMEM((rows, width), bf16),
            pltpu.SemaphoreType.DMA((SIDE + 16,)),
            pltpu.SemaphoreType.DMA((SIDE + 16,)),
            pltpu.SemaphoreType.DMA((nheads,)),
            pltpu.SemaphoreType.DMA((nheads,)),
            pltpu.SemaphoreType.DMA((3,)),
            pltpu.SemaphoreType.DMA((spans * heads,)),
        ],
        compiler_params=pltpu.CompilerParams(
            collective_id=0, has_side_effects=True, vmem_limit_bytes=60 * 2**20
        ),
        name="attend",
    )(doc_lengths, span_order, queries, keys, values)


def solution(mesh):
    return jax.shard_map(
        body,
        mesh=mesh,
        in_specs=(P("ctx", "head"), P("ctx", "head"), P("ctx", "head"), P(), P()),
        out_specs=P(("ctx", "head"), None),
        check_vma=False,
    )
```

```python
import math

import jax
import jax.numpy as jnp
from jax import lax
from jax.experimental import pallas as pl
from jax.experimental.pallas import tpu as pltpu
from jax.sharding import PartitionSpec as P

HD = 128
SPAN = 128
DEPTH = 8
CHUNK = 512
NCHUNK = 16
FAR = -(2.0**100)
RATE = math.log2(math.e) / math.sqrt(HD)
MESH = pl.DeviceIdType.MESH
VALS, KEYS, GUEST, FIRST, OVER, SIDE = 0, 7, 14, 21, 23, 30


def _pair(p, s, flip):
    return ((p, -s, flip), (p, s, flip))


ORDER = (
    ((0, 0, 0), (0, 0, 1)),
    _pair(0, 1, 0),
    ((1, 0, 0), (1, 0, 1)),
    _pair(0, 1, 1),
    _pair(0, 2, 0),
    _pair(1, 1, 0),
    _pair(0, 2, 1),
    _pair(1, 1, 1),
    _pair(0, 3, 0),
    _pair(1, 2, 0),
    _pair(0, 3, 1),
    _pair(1, 2, 1),
    _pair(1, 3, 0),
    _pair(1, 3, 1),
    ((0, 4, 0), (1, 4, 0)),
    ((0, 4, 1), (1, 4, 1)),
)


def kernel(
    lengths_ref, order_ref, q_ref, k_in, v_in, out_ref,
    buf, qa, acc, top, s0, s1, row_pos, row_start, o_st,
    send, recv, o_send, o_recv, here, q_sem,
):
    rows = k_in.shape[0]
    spans = rows // SPAN
    heads = q_ref.shape[1] // HD
    group = heads * SPAN
    width = q_ref.shape[1]
    nheads = lax.axis_size("head")
    share = rows // nheads
    ndocs = lengths_ref.shape[0]
    me = lax.axis_index("ctx")
    my_head = lax.axis_index("head")
    x, z, c = me // (2 * DEPTH), (me // 2) % DEPTH, me % 2
    sign = 1 - 2 * c

    def block(px, dz, flip):
        xx = x + px - 2 * x * px
        cc = c + flip - 2 * c * flip
        return xx * (2 * DEPTH) + ((z + dz + 2 * DEPTH) % DEPTH) * 2 + cc

    across, beside = block(1, 0, 0), block(0, 0, 1)
    hop = {0: block(0, 1, 0), 1: block(0, -1, 0)}
    far_to, far_from = block(0, sign, 0), {p: block(p, -3 * sign, 0) for p in (0, 1)}
    near = {
        (px, dz, f): block(px, dz, f) for px in (0, 1) for dz in range(-3, 5) for f in (0, 1)
    }

    barrier = pltpu.get_barrier_semaphore()
    for other in (*hop.values(), across, beside):
        pl.semaphore_signal(barrier, inc=1, device_id={"ctx": other}, device_id_type=MESH)
    for j in range(1, nheads):
        pl.semaphore_signal(
            barrier, inc=1, device_id={"head": lax.rem(my_head + j, nheads)}, device_id_type=MESH
        )

    K, V, KV = (0, rows), (rows, rows), (0, 2 * rows)

    def place(blk, part):
        return buf.at[pl.ds(pl.multiple_of(blk * (2 * rows) + part[0], rows), part[1])]

    stay = [
        pltpu.make_async_copy(k_in, place(me, K), here.at[0]),
        pltpu.make_async_copy(v_in, place(me, V), here.at[1]),
    ]
    asked = []
    for t in range(spans):
        for h in range(heads):
            asked.append(
                pltpu.make_async_copy(
                    q_ref.at[t * SPAN : (t + 1) * SPAN, h * HD : (h + 1) * HD],
                    qa.at[t * group + h * SPAN : t * group + (h + 1) * SPAN, 0:HD],
                    q_sem.at[t * heads + h],
                )
            )
    for copy in stay + asked:
        copy.start()

    sent = {}

    def put(blk, part, to, sem):
        place_there = place(blk, part)
        pltpu.make_async_remote_copy(
            src_ref=place_there,
            dst_ref=place_there,
            send_sem=send.at[sem],
            recv_sem=recv.at[sem],
            device_id={"ctx": to},
            device_id_type=MESH,
        ).start()
        sent[sem] = part

    def mirror(blk, part, sem):
        spot = place(blk, part)
        return pltpu.make_async_remote_copy(
            src_ref=spot,
            dst_ref=spot,
            send_sem=send.at[sem],
            recv_sem=recv.at[sem],
            device_id={"ctx": beside},
            device_id_type=MESH,
        )

    def got(blk, part, sem):
        mirror(blk, part, sem).wait_recv()

    ways = ((0, 1), (1, -1))

    def of(first, s, way):
        return first + (s - 1) * 2 + way

    RIDES = {"V": (0, V, VALS), "K": (0, K, KEYS), "P": (1, K, GUEST)}

    def ride(kind, s):
        p, part, first = RIDES[kind]
        if s == 4:
            got(near[p, 4, 0], part, first + 6)
            if kind == "V":
                put(near[0, 4, 0], V, across, OVER + 6)
            return
        for w, d in ways:
            blk = near[p, -s * d, 0]
            got(blk, part, of(first, s, w))
            if s < 3:
                put(blk, part, hop[w], of(first, s + 1, w))
        if s == 3:
            put(far_from[p], part, far_to, first + 6)
        if kind == "V":
            for w, d in ways:
                put(near[0, -s * d, 0], V, across, of(OVER, s, w))

    def pass_own(s):
        if s == 4:
            put(near[0, 4, 0], KV, beside, SIDE + 7)
            return
        for w, d in ways:
            put(near[0, -s * d, 0], KV, beside, SIDE + of(1, s, w))

    def guest_0():
        got(near[1, 0, 0], K, FIRST)
        for w, d in ways:
            put(near[1, 0, 0], K, hop[w], of(GUEST, 1, w))

    def other(s):
        if s == 0:
            got(near[1, 0, 0], V, FIRST + 1)
            put(near[1, 0, 0], KV, beside, SIDE + 8)
        elif s == 4:
            got(near[1, 4, 0], V, OVER + 6)
            put(near[1, 4, 0], KV, beside, SIDE + 8 + 7)
        else:
            for w, d in ways:
                blk = near[1, -s * d, 0]
                got(blk, V, of(OVER, s, w))
                put(blk, KV, beside, SIDE + 8 + of(1, s, w))

    def side(p, s):
        if s == 0:
            got(near[p, 0, 1], KV, SIDE + 8 * p)
        elif s == 4:
            got(near[p, 4, 1], KV, SIDE + 8 * p + 7)
        else:
            for w, d in ways:
                got(near[p, -d * s, 1], KV, SIDE + 8 * p + of(1, s, w))

    middle = {
        0: [guest_0, lambda: ride("V", 1), lambda: other(0), lambda: ride("K", 1), lambda: pass_own(1)],
        1: [lambda: side(1, 0)],
        2: [lambda: ride("P", 1), lambda: side(0, 1)],
        3: [lambda: ride("K", 2), lambda: pass_own(2)],
        4: [lambda: ride("P", 2)],
        5: [lambda: ride("V", 3), lambda: side(0, 2)],
        6: [lambda: side(1, 1)],
        7: [lambda: ride("V", 4)],
        8: [lambda: other(3)],
        9: [lambda: side(0, 3)],
        10: [lambda: ride("P", 4), lambda: other(4), lambda: side(1, 2)],
    }
    finish = {
        2: [lambda: ride("V", 2), lambda: other(1)],
        5: [lambda: ride("K", 3), lambda: other(2), lambda: pass_own(3)],
        6: [lambda: ride("P", 3)],
        7: [lambda: ride("K", 4), lambda: pass_own(4)],
        11: [lambda: side(1, 3)],
        12: [lambda: side(0, 4), lambda: side(1, 4)],
    }

    def chunk_blocks(m):
        def digit(code):
            return lax.rem(lax.shift_right_logical(jnp.int32(code), m), 2)

        found = []
        for i in range(2):
            px, far, flip = ([ORDER[n][i][f] for n in range(NCHUNK)] for f in range(3))
            dz = sum(
                (1 << e) * digit(sum(((v % DEPTH) >> e & 1) << n for n, v in enumerate(far)))
                for e in range(3)
            )
            code = [sum(v << n for n, v in enumerate(row)) for row in (px, flip)]
            found.append(block(digit(code[0]), dz, digit(code[1])))
        return found

    def keys_of(m, t):
        first, stop = row_start[pl.ds(t, 1), 0], row_pos[pl.ds(t, 1), 0]
        parts = []
        for blk in chunk_blocks(m):
            base = pl.multiple_of(blk * (2 * rows), 2 * rows)
            for i in range(spans):
                pos = order_ref[blk * spans + i] * SPAN + lax.broadcasted_iota(
                    jnp.int32, (SPAN, SPAN), 0
                )
                ok = (pos >= first) & (pos <= stop)
                hide = jnp.where(ok, 0.0, FAR).astype(jnp.bfloat16)
                parts.append(jnp.concatenate([buf[pl.ds(base + i * SPAN, SPAN)], hide], axis=1))
        return jnp.concatenate(parts, axis=0)

    def values_of(m):
        parts = []
        for blk in chunk_blocks(m):
            base = pl.multiple_of(blk * (2 * rows) + rows, rows)
            parts.append(
                jnp.concatenate([buf[pl.ds(base, rows)], jnp.ones((rows, HD), jnp.bfloat16)], axis=1)
            )
        return jnp.concatenate(parts, axis=0)

    def scores(m, t, dest):
        dest[...] = lax.dot_general(
            qa[pl.ds(pl.multiple_of(t * group, group), group)],
            keys_of(m, t),
            (((1,), (1,)), ((), ())),
            preferred_element_type=jnp.float32,
        )

    def fold(m, t, source):
        part = pl.ds(pl.multiple_of(t * group, group), group)
        score = source[...]
        old = top[part]
        new = jnp.maximum(old, jnp.max(score, axis=1, keepdims=True))
        weight = jnp.exp2((score - jnp.concatenate([new] * (CHUNK // HD), axis=1)) * RATE)
        factor = jnp.exp2((old - new) * RATE)
        made = jnp.dot(
            weight.astype(jnp.bfloat16), values_of(m), preferred_element_type=jnp.float32
        )
        top[part] = new
        acc[part] = acc[part] * jnp.concatenate([factor, factor], axis=1) + made

    def hand_out(t):
        for h in range(heads):
            part = slice(t * group + h * SPAN, t * group + (h + 1) * SPAN)
            done = acc[part, 0:HD] / acc[part, HD:]
            o_st[t * SPAN : (t + 1) * SPAN, h * HD : (h + 1) * HD] = done.astype(jnp.bfloat16)
        columns = pl.ds(pl.multiple_of(my_head * width, width), width)
        for r in range(SPAN // share):
            j = t * (SPAN // share) + r
            source = o_st.at[j * share : (j + 1) * share]

            @pl.when(my_head != j)
            def _():
                pltpu.make_async_remote_copy(
                    src_ref=source,
                    dst_ref=out_ref.at[:, columns],
                    send_sem=o_send.at[j],
                    recv_sem=o_recv.at[my_head],
                    device_id={"head": j},
                    device_id_type=MESH,
                ).start()

            @pl.when(my_head == j)
            def _():
                pltpu.make_async_copy(source, out_ref.at[:, columns], here.at[2]).start()

    eye = (
        lax.broadcasted_iota(jnp.int32, (SPAN, SPAN), 0)
        == lax.broadcasted_iota(jnp.int32, (SPAN, SPAN), 1)
    ).astype(jnp.bfloat16)
    for t in range(spans):
        pos = order_ref[me * spans + t] * SPAN + lax.broadcasted_iota(jnp.int32, (8, SPAN), 1)
        start, end = jnp.zeros((8, SPAN), jnp.int32), jnp.int32(0)
        for d in range(ndocs):
            end = end + lengths_ref[d]
            start = jnp.where(pos >= end, end, start)
        row_pos[t], row_start[t] = pos, start
        for h in range(heads):
            qa[t * group + h * SPAN : t * group + (h + 1) * SPAN, HD:] = eye
    acc[...] = jnp.zeros_like(acc)
    top[...] = jnp.full(top.shape, -1e30, jnp.float32)

    pl.semaphore_wait(barrier, 4 + nheads - 1)
    for copy in stay:
        copy.wait()
    put(me, K, across, FIRST)
    for w, d in ways:
        put(me, V, hop[w], of(VALS, 1, w))
    put(me, V, across, FIRST + 1)
    for w, d in ways:
        put(me, K, hop[w], of(KEYS, 1, w))
    put(me, KV, beside, SIDE)

    for copy in asked:
        copy.wait()

    side(0, 0)
    scores(0, 0, s0)

    @pl.loop(0, NCHUNK)
    def _(u):
        tail = u // 12
        v = (u - 12) * tail
        t_a = tail * (v // 2)
        t_b = 1 - tail + t_a
        m_a = (1 - tail) * u + tail * (12 + 2 * (v % 2))
        m_b = m_a + tail
        nxt = v + 1
        early = (1 - tail) * (u + 1)
        t_n = tail * ((nxt // 2) % 2)
        m_n = early + tail * (12 + 2 * (nxt % 2))
        scores(m_b, t_b, s1)
        fold(m_a, t_a, s0)
        for key, jobs in middle.items():

            @pl.when(u == key)
            def _(jobs=jobs):
                for job in jobs:
                    job()

        scores(m_n, t_n, s0)
        fold(m_b, t_b, s1)
        for key, jobs in finish.items():

            @pl.when(u == key)
            def _(jobs=jobs):
                for job in jobs:
                    job()

        @pl.when(u == 13)
        def _():
            hand_out(0)

    hand_out(1)
    for sem, part in sent.items():
        mirror(me, part, sem).wait_send()

    columns = pl.ds(pl.multiple_of(my_head * width, width), width)
    for j in range(nheads):
        source = o_st.at[j * share : (j + 1) * share]
        landing = pltpu.make_async_remote_copy(
            src_ref=source,
            dst_ref=out_ref.at[:, j * width : (j + 1) * width],
            send_sem=o_send.at[j],
            recv_sem=o_recv.at[j],
            device_id={"head": j},
            device_id_type=MESH,
        )

        @pl.when(my_head != j)
        def _():
            landing.wait_recv()
            landing.wait_send()

        @pl.when(my_head == j)
        def _():
            pltpu.make_async_copy(source, out_ref.at[:, columns], here.at[2]).wait()


def body(queries, keys, values, doc_lengths, span_order):
    rows, width = queries.shape
    heads, spans = width // HD, rows // SPAN
    n_ctx, nheads = lax.axis_size("ctx"), lax.axis_size("head")
    group = heads * SPAN
    smem, hbm = pl.BlockSpec(memory_space=pltpu.SMEM), pl.BlockSpec(memory_space=pltpu.HBM)
    f32, bf16, i32 = jnp.float32, jnp.bfloat16, jnp.int32
    return pl.pallas_call(
        kernel,
        out_shape=jax.ShapeDtypeStruct((rows // nheads, width * nheads), bf16),
        in_specs=[smem, smem, hbm, hbm, hbm],
        out_specs=hbm,
        scratch_shapes=[
            pltpu.VMEM((n_ctx * 2 * rows, HD), bf16),
            pltpu.VMEM((spans * group, 2 * HD), bf16),
            pltpu.VMEM((spans * group, 2 * HD), f32),
            pltpu.VMEM((spans * group, HD), f32),
            pltpu.VMEM((group, CHUNK), f32),
            pltpu.VMEM((group, CHUNK), f32),
            pltpu.VMEM((spans, 8, SPAN), i32),
            pltpu.VMEM((spans, 8, SPAN), i32),
            pltpu.VMEM((rows, width), bf16),
            pltpu.SemaphoreType.DMA((SIDE + 16,)),
            pltpu.SemaphoreType.DMA((SIDE + 16,)),
            pltpu.SemaphoreType.DMA((nheads,)),
            pltpu.SemaphoreType.DMA((nheads,)),
            pltpu.SemaphoreType.DMA((3,)),
            pltpu.SemaphoreType.DMA((spans * heads,)),
        ],
        compiler_params=pltpu.CompilerParams(
            collective_id=0, has_side_effects=True, vmem_limit_bytes=60 * 2**20
        ),
        name="attend",
    )(doc_lengths, span_order, queries, keys, values)


def solution(mesh):
    return jax.shard_map(
        body,
        mesh=mesh,
        in_specs=(P("ctx", "head"), P("ctx", "head"), P("ctx", "head"), P(), P()),
        out_specs=P(("ctx", "head"), None),
        check_vma=False,
    )
```

```python
import math

import jax
import jax.numpy as jnp
from jax import lax
from jax.experimental import pallas as pl
from jax.experimental.pallas import tpu as pltpu
from jax.sharding import PartitionSpec as P

HD = 128
SPAN = 128
DEPTH = 8
CHUNK = 512
NCHUNK = 16
FAR = -(2.0**100)
RATE = math.log2(math.e) / math.sqrt(HD)
MESH = pl.DeviceIdType.MESH
VALS, KEYS, GUEST, FIRST, OVER, SIDE = 0, 7, 14, 21, 23, 30


def _pair(p, s, flip):
    return ((p, -s, flip), (p, s, flip))


ORDER = (
    ((0, 0, 0), (0, 0, 1)),
    _pair(0, 1, 0),
    ((1, 0, 0), (1, 0, 1)),
    _pair(0, 1, 1),
    _pair(0, 2, 0),
    _pair(1, 1, 0),
    _pair(0, 2, 1),
    _pair(1, 1, 1),
    _pair(0, 3, 0),
    _pair(1, 2, 0),
    _pair(0, 3, 1),
    _pair(1, 2, 1),
    _pair(1, 3, 0),
    _pair(1, 3, 1),
    ((0, 4, 0), (1, 4, 0)),
    ((0, 4, 1), (1, 4, 1)),
)


def kernel(
    lengths_ref, order_ref, q_ref, k_in, v_in, out_ref,
    buf, qa, acc, top, s0, s1, row_pos, row_start, o_st,
    send, recv, o_send, o_recv, here, q_sem,
):
    rows = k_in.shape[0]
    spans = rows // SPAN
    heads = q_ref.shape[1] // HD
    group = heads * SPAN
    width = q_ref.shape[1]
    nheads = lax.axis_size("head")
    share = rows // nheads
    ndocs = lengths_ref.shape[0]
    me = lax.axis_index("ctx")
    my_head = lax.axis_index("head")
    x, z, c = me // (2 * DEPTH), (me // 2) % DEPTH, me % 2
    sign = 1 - 2 * c

    def block(px, dz, flip):
        xx = x + px - 2 * x * px
        cc = c + flip - 2 * c * flip
        return xx * (2 * DEPTH) + ((z + dz + 2 * DEPTH) % DEPTH) * 2 + cc

    across, beside = block(1, 0, 0), block(0, 0, 1)
    hop = {0: block(0, 1, 0), 1: block(0, -1, 0)}
    far_to, far_from = block(0, sign, 0), {p: block(p, -3 * sign, 0) for p in (0, 1)}
    near = {
        (px, dz, f): block(px, dz, f) for px in (0, 1) for dz in range(-3, 5) for f in (0, 1)
    }

    barrier = pltpu.get_barrier_semaphore()
    for other in (*hop.values(), across, beside):
        pl.semaphore_signal(barrier, inc=1, device_id={"ctx": other}, device_id_type=MESH)
    for j in range(1, nheads):
        pl.semaphore_signal(
            barrier, inc=1, device_id={"head": lax.rem(my_head + j, nheads)}, device_id_type=MESH
        )

    K, V, KV = (0, rows), (rows, rows), (0, 2 * rows)

    def place(blk, part):
        return buf.at[pl.ds(pl.multiple_of(blk * (2 * rows) + part[0], rows), part[1])]

    stay = [
        pltpu.make_async_copy(k_in, place(me, K), here.at[0]),
        pltpu.make_async_copy(v_in, place(me, V), here.at[1]),
    ]
    asked = []
    for t in range(spans):
        for h in range(heads):
            asked.append(
                pltpu.make_async_copy(
                    q_ref.at[t * SPAN : (t + 1) * SPAN, h * HD : (h + 1) * HD],
                    qa.at[t * group + h * SPAN : t * group + (h + 1) * SPAN, 0:HD],
                    q_sem.at[t * heads + h],
                )
            )
    for copy in stay + asked:
        copy.start()

    sent = {}

    def put(blk, part, to, sem):
        place_there = place(blk, part)
        pltpu.make_async_remote_copy(
            src_ref=place_there,
            dst_ref=place_there,
            send_sem=send.at[sem],
            recv_sem=recv.at[sem],
            device_id={"ctx": to},
            device_id_type=MESH,
        ).start()
        sent[sem] = part

    def mirror(blk, part, sem):
        spot = place(blk, part)
        return pltpu.make_async_remote_copy(
            src_ref=spot,
            dst_ref=spot,
            send_sem=send.at[sem],
            recv_sem=recv.at[sem],
            device_id={"ctx": beside},
            device_id_type=MESH,
        )

    def got(blk, part, sem):
        mirror(blk, part, sem).wait_recv()

    ways = ((0, 1), (1, -1))

    def of(first, s, way):
        return first + (s - 1) * 2 + way

    RIDES = {"V": (0, V, VALS), "K": (0, K, KEYS), "P": (1, K, GUEST)}

    def ride(kind, s):
        p, part, first = RIDES[kind]
        if s == 4:
            got(near[p, 4, 0], part, first + 6)
            if kind == "V":
                put(near[0, 4, 0], V, across, OVER + 6)
            return
        for w, d in ways:
            blk = near[p, -s * d, 0]
            got(blk, part, of(first, s, w))
            if s < 3:
                put(blk, part, hop[w], of(first, s + 1, w))
        if s == 3:
            put(far_from[p], part, far_to, first + 6)
        if kind == "V":
            for w, d in ways:
                put(near[0, -s * d, 0], V, across, of(OVER, s, w))

    def pass_own(s):
        if s == 4:
            put(near[0, 4, 0], KV, beside, SIDE + 7)
            return
        for w, d in ways:
            put(near[0, -s * d, 0], KV, beside, SIDE + of(1, s, w))

    def guest_0():
        got(near[1, 0, 0], K, FIRST)
        for w, d in ways:
            put(near[1, 0, 0], K, hop[w], of(GUEST, 1, w))

    def other(s):
        if s == 0:
            got(near[1, 0, 0], V, FIRST + 1)
            put(near[1, 0, 0], KV, beside, SIDE + 8)
        elif s == 4:
            got(near[1, 4, 0], V, OVER + 6)
            put(near[1, 4, 0], KV, beside, SIDE + 8 + 7)
        else:
            for w, d in ways:
                blk = near[1, -s * d, 0]
                got(blk, V, of(OVER, s, w))
                put(blk, KV, beside, SIDE + 8 + of(1, s, w))

    def side(p, s):
        if s == 0:
            got(near[p, 0, 1], KV, SIDE + 8 * p)
        elif s == 4:
            got(near[p, 4, 1], KV, SIDE + 8 * p + 7)
        else:
            for w, d in ways:
                got(near[p, -d * s, 1], KV, SIDE + 8 * p + of(1, s, w))

    middle = {
        0: [lambda: ride("V", 1), lambda: ride("K", 1), lambda: other(0), lambda: pass_own(1)],
        1: [lambda: side(1, 0)],
        2: [lambda: ride("P", 1), lambda: side(0, 1)],
        3: [lambda: ride("K", 2), lambda: pass_own(2)],
        4: [lambda: ride("P", 2)],
        5: [lambda: ride("V", 3), lambda: side(0, 2)],
        6: [lambda: side(1, 1)],
        7: [lambda: ride("V", 4)],
        8: [lambda: other(3)],
        9: [lambda: side(0, 3)],
        10: [lambda: ride("P", 4), lambda: other(4), lambda: side(1, 2)],
    }
    finish = {
        2: [lambda: ride("V", 2), lambda: other(1)],
        5: [lambda: ride("K", 3), lambda: other(2), lambda: pass_own(3)],
        6: [lambda: ride("P", 3)],
        7: [lambda: ride("K", 4), lambda: pass_own(4)],
        11: [lambda: side(1, 3)],
        12: [lambda: side(0, 4), lambda: side(1, 4)],
    }

    def chunk_blocks(m):
        def digit(code):
            return lax.rem(lax.shift_right_logical(jnp.int32(code), m), 2)

        found = []
        for i in range(2):
            px, far, flip = ([ORDER[n][i][f] for n in range(NCHUNK)] for f in range(3))
            dz = sum(
                (1 << e) * digit(sum(((v % DEPTH) >> e & 1) << n for n, v in enumerate(far)))
                for e in range(3)
            )
            code = [sum(v << n for n, v in enumerate(row)) for row in (px, flip)]
            found.append(block(digit(code[0]), dz, digit(code[1])))
        return found

    def keys_of(m, t):
        first, stop = row_start[pl.ds(t, 1), 0], row_pos[pl.ds(t, 1), 0]
        parts = []
        for blk in chunk_blocks(m):
            base = pl.multiple_of(blk * (2 * rows), 2 * rows)
            for i in range(spans):
                pos = order_ref[blk * spans + i] * SPAN + lax.broadcasted_iota(
                    jnp.int32, (SPAN, SPAN), 0
                )
                ok = (pos >= first) & (pos <= stop)
                hide = jnp.where(ok, 0.0, FAR).astype(jnp.bfloat16)
                parts.append(jnp.concatenate([buf[pl.ds(base + i * SPAN, SPAN)], hide], axis=1))
        return jnp.concatenate(parts, axis=0)

    def values_of(m):
        parts = []
        for blk in chunk_blocks(m):
            base = pl.multiple_of(blk * (2 * rows) + rows, rows)
            parts.append(
                jnp.concatenate([buf[pl.ds(base, rows)], jnp.ones((rows, HD), jnp.bfloat16)], axis=1)
            )
        return jnp.concatenate(parts, axis=0)

    def scores(m, t, dest):
        dest[...] = lax.dot_general(
            qa[pl.ds(pl.multiple_of(t * group, group), group)],
            keys_of(m, t),
            (((1,), (1,)), ((), ())),
            preferred_element_type=jnp.float32,
        )

    def fold(m, t, source):
        part = pl.ds(pl.multiple_of(t * group, group), group)
        score = source[...]
        old = top[part]
        new = jnp.maximum(old, jnp.max(score, axis=1, keepdims=True))
        weight = jnp.exp2((score - jnp.concatenate([new] * (CHUNK // HD), axis=1)) * RATE)
        factor = jnp.exp2((old - new) * RATE)
        made = jnp.dot(
            weight.astype(jnp.bfloat16), values_of(m), preferred_element_type=jnp.float32
        )
        top[part] = new
        acc[part] = acc[part] * jnp.concatenate([factor, factor], axis=1) + made

    def hand_out(t):
        for h in range(heads):
            part = slice(t * group + h * SPAN, t * group + (h + 1) * SPAN)
            done = acc[part, 0:HD] / acc[part, HD:]
            o_st[t * SPAN : (t + 1) * SPAN, h * HD : (h + 1) * HD] = done.astype(jnp.bfloat16)
        columns = pl.ds(pl.multiple_of(my_head * width, width), width)
        for r in range(SPAN // share):
            j = t * (SPAN // share) + r
            source = o_st.at[j * share : (j + 1) * share]

            @pl.when(my_head != j)
            def _():
                pltpu.make_async_remote_copy(
                    src_ref=source,
                    dst_ref=out_ref.at[:, columns],
                    send_sem=o_send.at[j],
                    recv_sem=o_recv.at[my_head],
                    device_id={"head": j},
                    device_id_type=MESH,
                ).start()

            @pl.when(my_head == j)
            def _():
                pltpu.make_async_copy(source, out_ref.at[:, columns], here.at[2]).start()

    eye = (
        lax.broadcasted_iota(jnp.int32, (SPAN, SPAN), 0)
        == lax.broadcasted_iota(jnp.int32, (SPAN, SPAN), 1)
    ).astype(jnp.bfloat16)
    for t in range(spans):
        pos = order_ref[me * spans + t] * SPAN + lax.broadcasted_iota(jnp.int32, (8, SPAN), 1)
        start, end = jnp.zeros((8, SPAN), jnp.int32), jnp.int32(0)
        for d in range(ndocs):
            end = end + lengths_ref[d]
            start = jnp.where(pos >= end, end, start)
        row_pos[t], row_start[t] = pos, start
        for h in range(heads):
            qa[t * group + h * SPAN : t * group + (h + 1) * SPAN, HD:] = eye
    acc[...] = jnp.zeros_like(acc)
    top[...] = jnp.full(top.shape, -1e30, jnp.float32)

    pl.semaphore_wait(barrier, 4 + nheads - 1)
    for copy in stay:
        copy.wait()
    put(me, K, across, FIRST)
    for w, d in ways:
        put(me, V, hop[w], of(VALS, 1, w))
    put(me, V, across, FIRST + 1)
    for w, d in ways:
        put(me, K, hop[w], of(KEYS, 1, w))
    put(me, KV, beside, SIDE)

    for copy in asked:
        copy.wait()

    guest_0()
    side(0, 0)
    scores(0, 0, s0)

    @pl.loop(0, NCHUNK)
    def _(u):
        tail = u // 12
        v = (u - 12) * tail
        t_a = tail * (v // 2)
        t_b = 1 - tail + t_a
        m_a = (1 - tail) * u + tail * (12 + 2 * (v % 2))
        m_b = m_a + tail
        nxt = v + 1
        early = (1 - tail) * (u + 1)
        t_n = tail * ((nxt // 2) % 2)
        m_n = early + tail * (12 + 2 * (nxt % 2))
        scores(m_b, t_b, s1)
        fold(m_a, t_a, s0)
        for key, jobs in middle.items():

            @pl.when(u == key)
            def _(jobs=jobs):
                for job in jobs:
                    job()

        scores(m_n, t_n, s0)
        fold(m_b, t_b, s1)
        for key, jobs in finish.items():

            @pl.when(u == key)
            def _(jobs=jobs):
                for job in jobs:
                    job()

        @pl.when(u == 13)
        def _():
            hand_out(0)

    hand_out(1)
    for sem, part in sent.items():
        mirror(me, part, sem).wait_send()

    columns = pl.ds(pl.multiple_of(my_head * width, width), width)
    for j in range(nheads):
        source = o_st.at[j * share : (j + 1) * share]
        landing = pltpu.make_async_remote_copy(
            src_ref=source,
            dst_ref=out_ref.at[:, j * width : (j + 1) * width],
            send_sem=o_send.at[j],
            recv_sem=o_recv.at[j],
            device_id={"head": j},
            device_id_type=MESH,
        )

        @pl.when(my_head != j)
        def _():
            landing.wait_recv()
            landing.wait_send()

        @pl.when(my_head == j)
        def _():
            pltpu.make_async_copy(source, out_ref.at[:, columns], here.at[2]).wait()


def body(queries, keys, values, doc_lengths, span_order):
    rows, width = queries.shape
    heads, spans = width // HD, rows // SPAN
    n_ctx, nheads = lax.axis_size("ctx"), lax.axis_size("head")
    group = heads * SPAN
    smem, hbm = pl.BlockSpec(memory_space=pltpu.SMEM), pl.BlockSpec(memory_space=pltpu.HBM)
    f32, bf16, i32 = jnp.float32, jnp.bfloat16, jnp.int32
    return pl.pallas_call(
        kernel,
        out_shape=jax.ShapeDtypeStruct((rows // nheads, width * nheads), bf16),
        in_specs=[smem, smem, hbm, hbm, hbm],
        out_specs=hbm,
        scratch_shapes=[
            pltpu.VMEM((n_ctx * 2 * rows, HD), bf16),
            pltpu.VMEM((spans * group, 2 * HD), bf16),
            pltpu.VMEM((spans * group, 2 * HD), f32),
            pltpu.VMEM((spans * group, HD), f32),
            pltpu.VMEM((group, CHUNK), f32),
            pltpu.VMEM((group, CHUNK), f32),
            pltpu.VMEM((spans, 8, SPAN), i32),
            pltpu.VMEM((spans, 8, SPAN), i32),
            pltpu.VMEM((rows, width), bf16),
            pltpu.SemaphoreType.DMA((SIDE + 16,)),
            pltpu.SemaphoreType.DMA((SIDE + 16,)),
            pltpu.SemaphoreType.DMA((nheads,)),
            pltpu.SemaphoreType.DMA((nheads,)),
            pltpu.SemaphoreType.DMA((3,)),
            pltpu.SemaphoreType.DMA((spans * heads,)),
        ],
        compiler_params=pltpu.CompilerParams(
            collective_id=0, has_side_effects=True, vmem_limit_bytes=60 * 2**20
        ),
        name="attend",
    )(doc_lengths, span_order, queries, keys, values)


def solution(mesh):
    return jax.shard_map(
        body,
        mesh=mesh,
        in_specs=(P("ctx", "head"), P("ctx", "head"), P("ctx", "head"), P(), P()),
        out_specs=P(("ctx", "head"), None),
        check_vma=False,
    )
```
